32 devices in a mesh: groups: 2 (over x), frag: 16 (over z, y, core).
Axes of the slice: x: 2, y: 2, z: 4, core: 2. Of those that a mesh axis runs over, the one named last changes fastest.
Arguments:
- density: bfloat16 [64, 512, 512], P(('groups', 'frag')), parts along dimension 0, may hold values from -2 to 2
- hcore: bfloat16 [64, 512, 512], P(('groups', 'frag')), parts along dimension 0, may hold values from -6 to 6
- kernel: bfloat16 [64, 512, 512], P(('groups', 'frag')), parts along dimension 0, may hold values from -0.25 to 0.25
- coupling: bfloat16 [64, 4, 512, 512], P(('groups', 'frag')), parts along dimension 0, may hold values from -0.25 to 0.25
- partners: int32 [32, 4], replicated, may hold values from 0 to 31, as said below
- pair_count: int32 [32], replicated, may hold values from 1 to 4
- charge_map: bfloat16 [64, 512, 128], P(('groups', 'frag')), parts along dimension 0, may hold values from -0.25 to 0.25
- charge_pos: float32 [64, 3, 128], P(('groups', 'frag')), parts along dimension 0, may hold values from 0 to 4
- grid_pos: float32 [64, 3, 256], P(('groups', 'frag')), parts along dimension 0, may hold values from 0 to 4
- grid_basis: bfloat16 [64, 512, 256], P(('groups', 'frag')), parts along dimension 0, may hold values from -0.375 to 0.375
Outputs:
- fock: float32 [64, 512, 512], P(('groups', 'frag')), parts along dimension 0
The draws below stay inside these ranges and needn't reach their ends.
There are 2 independent parts, one for each index of `groups`. The reference program is written for one: setup_inputs(seed, part) draws one part's arguments, and reference() takes and returns one part's arrays. A program takes and returns all parts, laid end to end along the dimension named above; an argument that names none is the same for every part. Nothing has to cross between parts.
Inputs may be any that keep to these rules, and one draw needn't show every extreme that they name: partners[I, k] is never I and lies on device I // 2 or on one of the two devices beside it, fragment F lying on device F // 2.
All inputs are finite; a program needn't handle non-finite values.
Results may differ from the reference program's by a relative error of at most 0.0028.
Values may be sent and summed in bfloat16 or wider, within the bound.
A program may use at most 192 MiB of HBM per device.

```python
import jax
import jax.numpy as jnp
from jax import lax

NB = 512
FPD = 2
KP = 4
QF = 128
GP = 256
NFRAG = 32


def draw_partners(key, part):
    key = jax.random.fold_in(key, 11)
    frag_ids = jnp.arange(NFRAG, dtype=jnp.int32)
    device = frag_ids // FPD
    lowest = jnp.maximum(device - 1, 0) * FPD
    highest = jnp.minimum(device + 2, NFRAG // FPD) * FPD
    spread = highest - lowest - 1
    picks = jax.random.randint(key, (NFRAG, KP), 0, 1 << 20, dtype=jnp.int32)
    chosen = lowest[:, None] + picks % spread[:, None]
    return chosen + (chosen >= frag_ids[:, None]).astype(jnp.int32)


def draw_pair_count(key, part):
    key = jax.random.fold_in(key, 23)
    counts = jax.random.randint(key, (NFRAG,), 1, KP + 1, dtype=jnp.int32)
    return counts.at[0].set(KP).at[NFRAG - 1].set(1)


def block_levels(own_key, extent, split, least, top_value):
    def one(position, blocks):
        draws = jax.random.uniform(jax.random.fold_in(jax.random.fold_in(own_key, 6), position), (blocks,), jnp.float32, least / len(split), top_value / len(split))
        return jnp.repeat(jnp.exp(draws), extent[position] // blocks).reshape((-1,) + (1,) * (len(extent) - position - 1))

    loudness = one(*split[0])
    for cut in split[1:]:
        loudness = loudness * one(*cut)
    return loudness


def noise(rng, dims, scale, bound, shards=(), kind=jnp.bfloat16):
    gain = block_levels(rng, dims, shards, -0.22, 0.18) if shards else 1.0
    result = jax.random.normal(rng, dims, jnp.float32) * scale * gain
    return jnp.minimum(jnp.maximum(result, -bound), bound).astype(kind)


def setup_inputs(seed: int = 0, part: int = 0) -> dict:
    key_of = jax.random.split(jax.random.key(seed), 11)
    own_keys = jax.random.split(jax.random.fold_in(key_of[10], part), 11)
    return {
        "density": noise(own_keys[0], (NFRAG, NB, NB), 0.25, 2.0, ((0, 16),)),
        "hcore": noise(own_keys[1], (NFRAG, NB, NB), 1.0, 6.0, ((0, 16),)),
        "kernel": noise(own_keys[2], (NFRAG, NB, NB), NB ** -0.5, 0.25, ((0, 16),)),
        "coupling": noise(own_keys[3], (NFRAG, KP, NB, NB), NB ** -0.5, 0.25, ((0, 16),)),
        "partners": draw_partners(jax.random.fold_in(key_of[10], 71), part),
        "pair_count": draw_pair_count(jax.random.fold_in(key_of[10], 71), part),
        "charge_map": noise(own_keys[6], (NFRAG, NB, QF), NB ** -0.5, 0.25, ((0, 16),)),
        "charge_pos": jnp.clip(4.0 * jax.random.uniform(own_keys[7], (NFRAG, 3, QF), jnp.float32) ** block_levels(own_keys[7], (NFRAG, 3, QF), ((0, 16),), -0.2, 0.2), 0.0, 4.0),
        "grid_pos": jnp.clip(4.0 * jax.random.uniform(own_keys[8], (NFRAG, 3, GP), jnp.float32) ** block_levels(own_keys[8], (NFRAG, 3, GP), ((0, 16),), -0.2, 0.2), 0.0, 4.0),
        "grid_basis": noise(own_keys[9], (NFRAG, NB, GP), GP ** -0.5, 0.375, ((0, 16),)),
    }


def potential_at(grid, owners, charges, places, sources):
    dist_sq = jnp.zeros((grid.shape[0], grid.shape[2], places.shape[0], places.shape[2]), jnp.float32)
    for coord in range(3):
        delta = grid[:, coord, :, None, None] - places[None, None, :, coord, :]
        dist_sq = dist_sq + delta * delta
    weights = charges[None, None, :, :] / jnp.sqrt(dist_sq + 1.0)
    keep = owners[:, None] != sources[None, :]
    weights = jnp.where(keep[:, None, :, None], weights, 0.0)
    return lax.optimization_barrier(jnp.sum(weights, axis=(2, 3)))

def reference(density, hcore, kernel, coupling, partners, pair_count, charge_map, charge_pos, grid_pos, grid_basis):
    populations = jnp.diagonal(density, axis1=1, axis2=2).astype(jnp.float32)
    charges = jnp.einsum('fm,fma->fa', populations, charge_map.astype(jnp.float32), precision=lax.Precision.HIGHEST)
    frag_ids = jnp.arange(NFRAG, dtype=jnp.int32)

    def one_field(items):
        grid, owner = items
        return potential_at(grid[None], owner[None], charges, charge_pos, frag_ids)[0]
    field = lax.map(one_field, (grid_pos, frag_ids))
    scaled = (grid_basis.astype(jnp.float32) * field[:, None, :]).astype(jnp.bfloat16)
    embed = jnp.einsum('fmg,fng->fmn', scaled.astype(jnp.float32), grid_basis.astype(jnp.float32))
    monomer = jnp.einsum('fmn,fnp->fmp', density.astype(jnp.float32), kernel.astype(jnp.float32))

    def add_dimers(totals, index):
        half_step = jnp.einsum('mn,knp->kmp', density[index].astype(jnp.float32), coupling[index].astype(jnp.float32)).astype(jnp.bfloat16)
        partner_dens = density[partners[index]].astype(jnp.float32)
        dimer = jnp.einsum('kmn,knp->kmp', half_step.astype(jnp.float32), partner_dens)
        live = (jnp.arange(KP, dtype=jnp.int32) < pair_count[index]).astype(jnp.float32)
        dimer = dimer * live[:, None, None]
        totals = totals.at[index].add(lax.optimization_barrier(jnp.sum(dimer, axis=0)))
        totals = totals.at[partners[index]].add(jnp.swapaxes(dimer, 1, 2))
        return (totals, None)
    start_totals = jnp.zeros((NFRAG, NB, NB), jnp.float32)
    totals, unused = lax.scan(add_dimers, start_totals, frag_ids)
    return hcore.astype(jnp.float32) + monomer + embed + totals
```

```python
import functools

import jax
import jax.numpy as jnp
from jax import lax
from jax.experimental import pallas as pl
from jax.experimental.pallas import tpu as pltpu
from jax.sharding import PartitionSpec as P

MESH = pl.DeviceIdType.MESH
F32 = jnp.float32
BF16 = jnp.bfloat16


def dot(a, b):
    return jnp.dot(a, b, preferred_element_type=F32)


def dot_t(a, b):
    return lax.dot_general(a, b, (((1,), (1,)), ((), ())), preferred_element_type=F32)


def fock_kernel(
    n, rows,
    partners, pair_count, density, hcore, kernel, coupling, charge_map, charge_pos, grid_pos, grid_basis,
    fock,
    win, coup, resp, core, cmap, gbas, half, t_send, t_recv, t_own, dens_t, acc, pub, every, place,
    in_sem, out_sem, d_send_sem, d_recv_sem, t_send_sem, t_recv_sem, q_send_sem, q_recv_sem,
):
    local, basis = density.shape[0], density.shape[1]
    slots = coupling.shape[1]
    points = grid_pos.shape[2]
    pieces = basis // rows
    group = lax.axis_index("groups")
    me = lax.axis_index("frag")
    first = me * local
    has_low, has_up = me > 0, me < n - 1

    loads = [
        pltpu.make_async_copy(density, win.at[pl.ds(local, local)], in_sem.at[0]),
        pltpu.make_async_copy(charge_map, cmap, in_sem.at[1]),
        pltpu.make_async_copy(coupling, coup, in_sem.at[2]),
        pltpu.make_async_copy(kernel, resp, in_sem.at[3]),
        pltpu.make_async_copy(hcore, core, in_sem.at[4]),
        pltpu.make_async_copy(grid_basis, gbas, in_sem.at[5]),
    ]
    for load in loads:
        load.start()

    barrier = pltpu.get_barrier_semaphore()

    def greet(step, carry):
        pl.semaphore_signal(
            barrier, inc=1, device_id=(group, lax.rem(me + step, n)), device_id_type=MESH
        )
        return carry

    lax.fori_loop(1, n, greet, 0)
    pl.semaphore_wait(barrier, n - 1)

    def dens_copy(side, f):
        return pltpu.make_async_remote_copy(
            src_ref=density.at[f],
            dst_ref=win.at[f if side == 0 else 2 * local + f],
            send_sem=d_send_sem.at[side, f],
            recv_sem=d_recv_sem.at[side, f],
            device_id=(group, me + 1 if side == 0 else me - 1),
            device_id_type=MESH,
        )

    def term_copy(side, f, c):
        part = pl.ds(pl.multiple_of(c * rows, rows), rows)
        return pltpu.make_async_remote_copy(
            src_ref=t_send.at[side, f, part],
            dst_ref=t_recv.at[side, f, part],
            send_sem=t_send_sem.at[side, f, c],
            recv_sem=t_recv_sem.at[side, f, c],
            device_id=(group, me + 1 if side == 0 else me - 1),
            device_id_type=MESH,
        )

    sends_to = (has_up, has_low)
    gets_from = (has_low, has_up)
    for side in range(2):
        @pl.when(sends_to[side])
        def _():
            for f in range(local):
                dens_copy(side, f).start()

    loads[0].wait()
    loads[1].wait()
    edge = 128
    eye = lax.broadcasted_iota(jnp.int32, (edge, edge), 0) == lax.broadcasted_iota(
        jnp.int32, (edge, edge), 1
    )
    for f in range(local):
        total = jnp.zeros((1, cmap.shape[2]), F32)
        for b in range(basis // edge):
            span = pl.ds(b * edge, edge)
            block = win[local + f, span, span].astype(F32)
            pops = jnp.sum(jnp.where(eye, block, 0.0), axis=1, keepdims=True)
            total = total + jnp.sum(pops * cmap[f, span, :].astype(F32), axis=0, keepdims=True)
        pub[f, 0:1, :] = total
        pub[f, 1:4, :] = charge_pos[f]
    every[me] = pub[...]

    def publish(step):
        target = lax.rem(me + step, n)
        return pltpu.make_async_remote_copy(
            src_ref=pub,
            dst_ref=every.at[me],
            send_sem=q_send_sem.at[step],
            recv_sem=q_recv_sem.at[step],
            device_id=(group, target),
            device_id_type=MESH,
        )

    def publish_start(step, carry):
        publish(step).start()
        return carry

    lax.fori_loop(1, n, publish_start, 0)

    loads[2].wait()
    live, position = [], []
    for f in range(local):
        count = pair_count[first + f]
        for k in range(slots):
            live.append(jnp.where(k < count, 1.0, 0.0).astype(F32))
            position.append(partners[first + f, k] - (me - 1) * local)
    for f in range(local):
        for k in range(slots):
            half[f * slots + k] = (
                dot(win[local + f], coup[f, k]) * live[f * slots + k]
            ).astype(BF16)

    weights = [
        [jnp.where(p == w, 1.0, 0.0).astype(F32) for p in position] for w in range(3 * local)
    ]

    def gather_terms(step, carry):
        span = pl.ds(pl.multiple_of(step * 32, 32), 32)
        for c in range(basis // 128):
            cols = pl.ds(c * 128, 128)
            pieces_here = [half[i, span, cols].astype(F32) for i in range(local * slots)]
            for w in range(3 * local):
                value = pieces_here[0] * weights[w][0]
                for i in range(1, local * slots):
                    value = value + pieces_here[i] * weights[w][i]
                value = value.astype(BF16)
                if w < local:
                    t_send[1, w, span, cols] = value
                elif w < 2 * local:
                    t_own[w - local, span, cols] = value
                else:
                    t_send[0, w - 2 * local, span, cols] = value
        return carry

    per_piece = rows // 32
    for c in range(pieces):
        lax.fori_loop(c * per_piece, (c + 1) * per_piece, gather_terms, 0)
        for side in range(2):
            @pl.when(sends_to[side])
            def _():
                for f in range(local):
                    term_copy(side, f, c).start()

    loads[3].wait()
    loads[4].wait()
    for f in range(local):
        own = win[local + f]
        dens_t[f] = own.T
        acc[f] = core[f].astype(F32) + dot(own, resp[f])
        acc[f] += dot_t(dens_t[f], t_own[f])

    def publish_wait(step, carry):
        publish(step).wait()
        return carry

    lax.fori_loop(1, n, publish_wait, 0)
    loads[5].wait()
    for f in range(local):
        for axis in range(3):
            place[axis] = jnp.broadcast_to(grid_pos[f, axis : axis + 1, :], (128, points)).T

        field_parts = []
        strip = 64
        for g in range(points // strip):
            span = pl.ds(g * strip, strip)
            px, py, pz = (place[axis, span, :] for axis in range(3))

            def add_source(source, total):
                for other in range(local):
                    keep = jnp.where(source * local + other == first + f, 0.0, 1.0).astype(F32)
                    rowsof = every[source, other]
                    dx = px - rowsof[1:2]
                    dy = py - rowsof[2:3]
                    dz = pz - rowsof[3:4]
                    total = total + (rowsof[0:1] * keep) * lax.rsqrt(
                        dx * dx + dy * dy + dz * dz + 1.0
                    )
                return total

            field_parts.append(lax.fori_loop(0, n, add_source, jnp.zeros((strip, 128), F32)))
        total = jnp.concatenate(field_parts, axis=0)
        field = jnp.sum(total.T, axis=0, keepdims=True)
        scaled = (gbas[f].astype(F32) * field).astype(BF16)
        acc[f] += dot_t(scaled, gbas[f])

    for side in range(2):
        @pl.when(gets_from[side])
        def _():
            for f in range(local):
                dens_copy(side, f).wait_recv()
    for f in range(local):
        for k in range(slots):
            where = jnp.clip(position[f * slots + k], 0, 3 * local - 1)
            acc[f] += dot(half[f * slots + k], win[where])

    for f in range(local):
        def add_piece(c, carry):
            part = pl.ds(pl.multiple_of(c * rows, rows), rows)
            for side in range(2):
                @pl.when(gets_from[side])
                def _():
                    term_copy(side, f, c).wait_recv()
                    acc[f, :, part] += dot_t(dens_t[f], t_recv[side, f, part, :])
            return carry

        lax.fori_loop(0, pieces, add_piece, 0)
        pltpu.make_async_copy(acc.at[f], fock.at[f], out_sem.at[f]).start()

    for side in range(2):
        @pl.when(sends_to[side])
        def _():
            for f in range(local):
                dens_copy(side, f).wait_send()
                for c in range(pieces):
                    term_copy(side, f, c).wait_send()
    for f in range(local):
        pltpu.make_async_copy(acc.at[f], fock.at[f], out_sem.at[f]).wait()


def body(
    density, hcore, kernel, coupling, partners, pair_count, charge_map, charge_pos, grid_pos, grid_basis
):
    n = lax.axis_size("frag")
    local, basis, _ = density.shape
    slots = coupling.shape[1]
    points = grid_pos.shape[2]
    charges = charge_map.shape[2]
    rows = 128
    pieces = basis // rows
    anywhere = pl.BlockSpec(memory_space=pl.ANY)
    smem = pl.BlockSpec(memory_space=pltpu.SMEM)
    vmem = pl.BlockSpec(memory_space=pltpu.VMEM)
    square = (basis, basis)
    dma = pltpu.SemaphoreType.DMA
    return pl.pallas_call(
        functools.partial(fock_kernel, n, rows),
        out_shape=jax.ShapeDtypeStruct((local,) + square, F32),
        in_specs=[smem, smem, anywhere, anywhere, anywhere, anywhere, anywhere, vmem, vmem, anywhere],
        out_specs=anywhere,
        scratch_shapes=[
            pltpu.VMEM((3 * local,) + square, BF16),
            pltpu.VMEM((local, slots) + square, BF16),
            pltpu.VMEM((local,) + square, BF16),
            pltpu.VMEM((local,) + square, BF16),
            pltpu.VMEM((local, basis, charges), BF16),
            pltpu.VMEM((local, basis, points), BF16),
            pltpu.VMEM((local * slots,) + square, BF16),
            pltpu.VMEM((2, local) + square, BF16),
            pltpu.VMEM((2, local) + square, BF16),
            pltpu.VMEM((local,) + square, BF16),
            pltpu.VMEM((local,) + square, BF16),
            pltpu.VMEM((local,) + square, F32),
            pltpu.VMEM((local, 4, charges), F32),
            pltpu.VMEM((n, local, 4, charges), F32),
            pltpu.VMEM((3, points, 128), F32),
            dma((6,)),
            dma((local,)),
            dma((2, local)),
            dma((2, local)),
            dma((2, local, pieces)),
            dma((2, local, pieces)),
            dma((n,)),
            dma((n,)),
        ],
        compiler_params=pltpu.CompilerParams(
            collective_id=0, has_side_effects=True, vmem_limit_bytes=48 * 1024 * 1024
        ),
    )(partners, pair_count, density, hcore, kernel, coupling, charge_map, charge_pos, grid_pos, grid_basis)


def solution(mesh):
    split = ("groups", "frag")
    block = P(split, None, None)
    in_specs = (
        block, block, block, P(split, None, None, None), P(), P(), block, block, block, block,
    )
    return jax.shard_map(body, mesh=mesh, in_specs=in_specs, out_specs=block, check_vma=False)
```

```python
import functools

import jax
import jax.numpy as jnp
from jax import lax
from jax.experimental import pallas as pl
from jax.experimental.pallas import tpu as pltpu
from jax.sharding import PartitionSpec as P

MESH = pl.DeviceIdType.MESH
F32 = jnp.float32
BF16 = jnp.bfloat16


def dot(a, b):
    return jnp.dot(a, b, preferred_element_type=F32)


def dot_t(a, b):
    return lax.dot_general(a, b, (((1,), (1,)), ((), ())), preferred_element_type=F32)


def fock_kernel(
    n, rows,
    partners_in, counts_in, density, hcore, kernel, coupling, charge_map, charge_pos, grid_pos, grid_basis,
    fock,
    win, coup, resp, core, cmap, gbas, half, t_send, t_recv, t_own, dens_t, acc, pub, every, place,
    relay, cpos, gpos, partners, pair_count,
    in_sem, out_sem, d_send_sem, d_recv_sem, t_send_sem, t_recv_sem, q_send_sem, q_recv_sem,
    divert_sem, relay_sem, forward_sem,
):
    local, basis = density.shape[0], density.shape[1]
    slots = coupling.shape[1]
    points = grid_pos.shape[2]
    pieces = basis // rows
    group = lax.axis_index("groups")
    me = lax.axis_index("frag")
    first = me * local
    has_low, has_up = me > 0, me < n - 1

    loads = [
        pltpu.make_async_copy(density, win.at[pl.ds(local, local)], in_sem.at[0]),
        pltpu.make_async_copy(charge_map, cmap, in_sem.at[1]),
        pltpu.make_async_copy(coupling, coup, in_sem.at[2]),
        pltpu.make_async_copy(kernel, resp, in_sem.at[3]),
        pltpu.make_async_copy(hcore, core, in_sem.at[4]),
        pltpu.make_async_copy(grid_basis, gbas, in_sem.at[5]),
        pltpu.make_async_copy(charge_pos, cpos, in_sem.at[6]),
        pltpu.make_async_copy(grid_pos, gpos, in_sem.at[7]),
        pltpu.make_async_copy(partners_in, partners, in_sem.at[8]),
        pltpu.make_async_copy(counts_in, pair_count, in_sem.at[9]),
    ]
    for load in loads:
        load.start()

    barrier = pltpu.get_barrier_semaphore()

    def greet(step, carry):
        pl.semaphore_signal(
            barrier, inc=1, device_id=(group, lax.rem(me + step, n)), device_id_type=MESH
        )
        return carry

    lax.fori_loop(1, n, greet, 0)
    pl.semaphore_wait(barrier, n - 1)

    def dens_copy(side, f):
        return pltpu.make_async_remote_copy(
            src_ref=density.at[f],
            dst_ref=win.at[f if side == 0 else 2 * local + f],
            send_sem=d_send_sem.at[side, f],
            recv_sem=d_recv_sem.at[side, f],
            device_id=(group, me + 1 if side == 0 else me - 1),
            device_id_type=MESH,
        )

    def term_copy(side, f, c):
        part = pl.ds(pl.multiple_of(c * rows, rows), rows)
        return pltpu.make_async_remote_copy(
            src_ref=t_send.at[side, f, part],
            dst_ref=t_recv.at[side, f, part],
            send_sem=t_send_sem.at[side, f, c],
            recv_sem=t_recv_sem.at[side, f, c],
            device_id=(group, me + 1 if side == 0 else me - 1),
            device_id_type=MESH,
        )

    sends_to = (has_up, has_low)
    gets_from = (has_low, has_up)

    place_in, layer = lax.rem(me, 4), lax.div(me, 4)

    def diverted(side, i):
        if n != 16 or local != 2 or i > 2:
            return None
        if side == 0:
            return jnp.logical_and(place_in == 3, i < 3 - layer)
        return jnp.logical_and(place_in == 0, i < layer)

    def relays(side, i):
        if n != 16 or local != 2 or i > 2:
            return None
        if side == 0:
            return jnp.logical_and(place_in == 0, i < 3 - layer)
        return jnp.logical_and(place_in == 3, i < layer)

    def direct(side, i):
        away = diverted(side, i)
        if away is None:
            return sends_to[side]
        return jnp.logical_and(sends_to[side], jnp.logical_not(away))

    def divert_copy(side, i, c):
        part = pl.ds(c * rows, rows)
        return pltpu.make_async_remote_copy(
            src_ref=density.at[i, part] if i < local else t_send.at[side, i - local, part],
            dst_ref=relay.at[i, part],
            send_sem=divert_sem.at[i, c],
            recv_sem=relay_sem.at[i, c],
            device_id=(group, me - 3 if side == 0 else me + 3),
            device_id_type=MESH,
        )

    def forward_copy(side, i, c):
        part = pl.ds(c * rows, rows)
        if i < local:
            target = win.at[i if side == 0 else 2 * local + i, part]
            arrived = d_recv_sem.at[side, i]
        else:
            target = t_recv.at[side, i - local, part]
            arrived = t_recv_sem.at[side, i - local, c]
        return pltpu.make_async_remote_copy(
            src_ref=relay.at[i, part],
            dst_ref=target,
            send_sem=forward_sem.at[i, c],
            recv_sem=arrived,
            device_id=(group, me + 4 if side == 0 else me - 4),
            device_id_type=MESH,
        )

    def pass_on(i):
        for side in range(2):
            if relays(side, i) is not None:
                @pl.when(relays(side, i))
                def _():
                    for c in range(pieces):
                        divert_copy(side, i, c).wait_recv()
                        forward_copy(side, i, c).start()

    for f in range(local):
        for side in range(2):
            if diverted(side, f) is not None:
                @pl.when(diverted(side, f))
                def _():
                    for c in range(pieces):
                        divert_copy(side, f, c).start()

            @pl.when(direct(side, f))
            def _():
                dens_copy(side, f).start()

    loads[0].wait()
    loads[1].wait()
    loads[6].wait()
    edge = 128
    eye = lax.broadcasted_iota(jnp.int32, (edge, edge), 0) == lax.broadcasted_iota(
        jnp.int32, (edge, edge), 1
    )
    for f in range(local):
        total = jnp.zeros((1, cmap.shape[2]), F32)
        for b in range(basis // edge):
            span = pl.ds(b * edge, edge)
            block = win[local + f, span, span].astype(F32)
            pops = jnp.sum(jnp.where(eye, block, 0.0), axis=1, keepdims=True)
            total = total + jnp.sum(pops * cmap[f, span, :].astype(F32), axis=0, keepdims=True)
        pub[f, 0:1, :] = total
        pub[f, 1:4, :] = cpos[:, f, :]
    every[me] = pub[...]

    def publish(step):
        target = lax.rem(me + step, n)
        return pltpu.make_async_remote_copy(
            src_ref=pub,
            dst_ref=every.at[me],
            send_sem=q_send_sem.at[step],
            recv_sem=q_recv_sem.at[step],
            device_id=(group, target),
            device_id_type=MESH,
        )

    def publish_start(step, carry):
        publish(step).start()
        return carry

    lax.fori_loop(1, n, publish_start, 0)

    loads[2].wait()
    loads[8].wait()
    loads[9].wait()
    live, position = [], []
    for f in range(local):
        count = pair_count[first + f]
        for k in range(slots):
            live.append(jnp.where(k < count, 1.0, 0.0).astype(F32))
            position.append(partners[k, first + f] - (me - 1) * local)
    for f in range(local):
        for k in range(slots):
            half[f * slots + k] = (
                dot(win[local + f], coup[f, k]) * live[f * slots + k]
            ).astype(BF16)

    weights = [
        [jnp.where(p == w, 1.0, 0.0).astype(F32) for p in position] for w in range(3 * local)
    ]

    def gather_terms(step, carry):
        span = pl.ds(pl.multiple_of(step * 32, 32), 32)
        for c in range(basis // 128):
            cols = pl.ds(c * 128, 128)
            pieces_here = [half[i, span, cols].astype(F32) for i in range(local * slots)]
            for w in range(3 * local):
                value = pieces_here[0] * weights[w][0]
                for i in range(1, local * slots):
                    value = value + pieces_here[i] * weights[w][i]
                value = value.astype(BF16)
                if w < local:
                    t_send[1, w, span, cols] = value
                elif w < 2 * local:
                    t_own[w - local, span, cols] = value
                else:
                    t_send[0, w - 2 * local, span, cols] = value
        return carry

    lax.fori_loop(0, basis // 32, gather_terms, 0)

    def send_terms(f):
        for side in range(2):
            if diverted(side, local + f) is not None:
                @pl.when(diverted(side, local + f))
                def _():
                    for c in range(pieces):
                        divert_copy(side, local + f, c).start()

            @pl.when(direct(side, local + f))
            def _():
                for c in range(pieces):
                    term_copy(side, f, c).start()

    pass_on(0)
    late = relays(0, 1)
    for f in range(local):
        if late is None or f == 0:
            send_terms(f)
    if late is not None:
        late = jnp.logical_or(late, relays(1, 1))

        @pl.when(jnp.logical_not(late))
        def _():
            send_terms(1)

    loads[3].wait()
    loads[4].wait()
    for f in range(local):
        own = win[local + f]
        dens_t[f] = own.T
        acc[f] = core[f].astype(F32) + dot(own, resp[f])
        acc[f] += dot_t(dens_t[f], t_own[f])

    def publish_wait(step, carry):
        publish(step).wait()
        return carry

    pass_on(1)
    if late is not None:
        @pl.when(late)
        def _():
            send_terms(1)
    lax.fori_loop(1, n, publish_wait, 0)
    loads[5].wait()
    loads[7].wait()
    for f in range(local):
        for axis in range(3):
            place[axis] = jnp.broadcast_to(gpos[axis, f : f + 1, :], (128, points)).T

        field_parts = []
        strip = 64
        for g in range(points // strip):
            span = pl.ds(g * strip, strip)
            px, py, pz = (place[axis, span, :] for axis in range(3))

            def add_source(source, total):
                for other in range(local):
                    keep = jnp.where(source * local + other == first + f, 0.0, 1.0).astype(F32)
                    rowsof = every[source, other]
                    dx = px - rowsof[1:2]
                    dy = py - rowsof[2:3]
                    dz = pz - rowsof[3:4]
                    total = total + (rowsof[0:1] * keep) * lax.rsqrt(
                        dx * dx + dy * dy + dz * dz + 1.0
                    )
                return total

            field_parts.append(lax.fori_loop(0, n, add_source, jnp.zeros((strip, 128), F32)))
        total = jnp.concatenate(field_parts, axis=0)
        field = jnp.sum(total.T, axis=0, keepdims=True)
        scaled = (gbas[f].astype(F32) * field).astype(BF16)
        acc[f] += dot_t(scaled, gbas[f])

    pass_on(2)

    for side in range(2):
        @pl.when(gets_from[side])
        def _():
            for f in range(local):
                dens_copy(side, f).wait_recv()
    for f in range(local):
        for k in range(slots):
            where = jnp.clip(position[f * slots + k], 0, 3 * local - 1)
            acc[f] += dot(half[f * slots + k], win[where])

    for f in range(local):
        def add_piece(c, carry):
            part = pl.ds(pl.multiple_of(c * rows, rows), rows)
            for side in range(2):
                @pl.when(gets_from[side])
                def _():
                    term_copy(side, f, c).wait_recv()
                    acc[f, :, part] += dot_t(dens_t[f], t_recv[side, f, part, :])
            return carry

        lax.fori_loop(0, pieces, add_piece, 0)
        pltpu.make_async_copy(acc.at[f], fock.at[f], out_sem.at[f]).start()

    for side in range(2):
        for i in range(2 * local):
            @pl.when(direct(side, i))
            def _():
                if i < local:
                    dens_copy(side, i).wait_send()
                else:
                    for c in range(pieces):
                        term_copy(side, i - local, c).wait_send()

            if diverted(side, i) is not None:
                @pl.when(diverted(side, i))
                def _():
                    for c in range(pieces):
                        divert_copy(side, i, c).wait_send()

                @pl.when(relays(side, i))
                def _():
                    for c in range(pieces):
                        forward_copy(side, i, c).wait_send()
    for f in range(local):
        pltpu.make_async_copy(acc.at[f], fock.at[f], out_sem.at[f]).wait()


def body(
    density, hcore, kernel, coupling, partners, pair_count, charge_map, charge_pos, grid_pos, grid_basis
):
    n = lax.axis_size("frag")
    local, basis, _ = density.shape
    slots = coupling.shape[1]
    points = grid_pos.shape[2]
    charges = charge_map.shape[2]
    rows = 128
    pieces = basis // rows
    hbm = pl.BlockSpec(memory_space=pltpu.HBM)
    square = (basis, basis)
    dma = pltpu.SemaphoreType.DMA
    return pl.pallas_call(
        functools.partial(fock_kernel, n, rows),
        out_shape=jax.ShapeDtypeStruct((local,) + square, F32),
        in_specs=[hbm] * 10,
        out_specs=hbm,
        scratch_shapes=[
            pltpu.VMEM((3 * local,) + square, BF16),
            pltpu.VMEM((local, slots) + square, BF16),
            pltpu.VMEM((local,) + square, BF16),
            pltpu.VMEM((local,) + square, BF16),
            pltpu.VMEM((local, basis, charges), BF16),
            pltpu.VMEM((local, basis, points), BF16),
            pltpu.VMEM((local * slots,) + square, BF16),
            pltpu.VMEM((2, local) + square, BF16),
            pltpu.VMEM((2, local) + square, BF16),
            pltpu.VMEM((local,) + square, BF16),
            pltpu.VMEM((local,) + square, BF16),
            pltpu.VMEM((local,) + square, F32),
            pltpu.VMEM((local, 4, charges), F32),
            pltpu.VMEM((n, local, 4, charges), F32),
            pltpu.VMEM((3, points, 128), F32),
            pltpu.VMEM((3,) + square, BF16),
            pltpu.VMEM((3, local, charges), F32),
            pltpu.VMEM((3, local, points), F32),
            pltpu.SMEM(partners.shape[::-1], jnp.int32),
            pltpu.SMEM(pair_count.shape, jnp.int32),
            dma((10,)),
            dma((local,)),
            dma((2, local)),
            dma((2, local)),
            dma((2, local, pieces)),
            dma((2, local, pieces)),
            dma((n,)),
            dma((n,)),
            dma((3, pieces)),
            dma((3, pieces)),
            dma((3, pieces)),
        ],
        compiler_params=pltpu.CompilerParams(
            collective_id=0, has_side_effects=True, vmem_limit_bytes=63 * 1024 * 1024
        ),
    )(partners.T, pair_count, density, hcore, kernel, coupling, charge_map,
      jnp.swapaxes(charge_pos, 0, 1), jnp.swapaxes(grid_pos, 0, 1), grid_basis)


def solution(mesh):
    split = ("groups", "frag")
    block = P(split, None, None)
    in_specs = (
        block, block, block, P(split, None, None, None), P(), P(), block, block, block, block,
    )
    return jax.shard_map(body, mesh=mesh, in_specs=in_specs, out_specs=block, check_vma=False)
```

```python
import functools

import jax
import jax.numpy as jnp
from jax import lax
from jax.experimental import pallas as pl
from jax.experimental.pallas import tpu as pltpu
from jax.sharding import PartitionSpec as P

MESH = pl.DeviceIdType.MESH
F32 = jnp.float32
BF16 = jnp.bfloat16


def dot(a, b):
    return jnp.dot(a, b, preferred_element_type=F32)


def dot_t(a, b):
    return lax.dot_general(a, b, (((1,), (1,)), ((), ())), preferred_element_type=F32)


def fock_kernel(
    n, rows,
    partners_in, counts_in, density, hcore, kernel, coupling, charge_map, charge_pos, grid_pos, grid_basis,
    fock,
    win, coup, resp, core, cmap, gbas, half, t_send, t_recv, t_own, dens_t, acc, pub, every, place,
    relay, cpos, gpos, partners, pair_count,
    in_sem, out_sem, d_send_sem, d_recv_sem, t_send_sem, t_recv_sem, q_send_sem, q_recv_sem,
    divert_sem, relay_sem, forward_sem,
):
    local, basis = density.shape[0], density.shape[1]
    slots = coupling.shape[1]
    points = grid_pos.shape[2]
    pieces = basis // rows
    group = lax.axis_index("groups")
    me = lax.axis_index("frag")
    first = me * local
    has_low, has_up = me > 0, me < n - 1

    loads = [
        pltpu.make_async_copy(density, win.at[pl.ds(local, local)], in_sem.at[0]),
        pltpu.make_async_copy(charge_map, cmap, in_sem.at[1]),
        pltpu.make_async_copy(coupling, coup, in_sem.at[2]),
        pltpu.make_async_copy(kernel, resp, in_sem.at[3]),
        pltpu.make_async_copy(hcore, core, in_sem.at[4]),
        pltpu.make_async_copy(grid_basis, gbas, in_sem.at[5]),
        pltpu.make_async_copy(charge_pos, cpos, in_sem.at[6]),
        pltpu.make_async_copy(grid_pos, gpos, in_sem.at[7]),
        pltpu.make_async_copy(partners_in, partners, in_sem.at[8]),
        pltpu.make_async_copy(counts_in, pair_count, in_sem.at[9]),
    ]
    for load in loads:
        load.start()

    barrier = pltpu.get_barrier_semaphore()

    def greet(step, carry):
        pl.semaphore_signal(
            barrier, inc=1, device_id=(group, lax.rem(me + step, n)), device_id_type=MESH
        )
        return carry

    lax.fori_loop(1, n, greet, 0)
    pl.semaphore_wait(barrier, n - 1)

    def dens_copy(side, f):
        return pltpu.make_async_remote_copy(
            src_ref=density.at[f],
            dst_ref=win.at[f if side == 0 else 2 * local + f],
            send_sem=d_send_sem.at[side, f],
            recv_sem=d_recv_sem.at[side, f],
            device_id=(group, me + 1 if side == 0 else me - 1),
            device_id_type=MESH,
        )

    def term_copy(side, f, c):
        part = pl.ds(pl.multiple_of(c * rows, rows), rows)
        return pltpu.make_async_remote_copy(
            src_ref=t_send.at[side, f, part],
            dst_ref=t_recv.at[side, f, part],
            send_sem=t_send_sem.at[side, f, c],
            recv_sem=t_recv_sem.at[side, f, c],
            device_id=(group, me + 1 if side == 0 else me - 1),
            device_id_type=MESH,
        )

    sends_to = (has_up, has_low)
    gets_from = (has_low, has_up)

    place_in, layer = lax.rem(me, 4), lax.div(me, 4)

    def diverted(side, i):
        if n != 16 or local != 2 or i > 2:
            return None
        if side == 0:
            return jnp.logical_and(place_in == 3, i < 3 - layer)
        return jnp.logical_and(place_in == 0, i < layer)

    def relays(side, i):
        if n != 16 or local != 2 or i > 2:
            return None
        if side == 0:
            return jnp.logical_and(place_in == 0, i < 3 - layer)
        return jnp.logical_and(place_in == 3, i < layer)

    def direct(side, i):
        away = diverted(side, i)
        if away is None:
            return sends_to[side]
        return jnp.logical_and(sends_to[side], jnp.logical_not(away))

    def divert_copy(side, i, c):
        part = pl.ds(c * rows, rows)
        return pltpu.make_async_remote_copy(
            src_ref=density.at[i, part] if i < local else t_send.at[side, i - local, part],
            dst_ref=relay.at[i, part],
            send_sem=divert_sem.at[i, c],
            recv_sem=relay_sem.at[i, c],
            device_id=(group, me - 3 if side == 0 else me + 3),
            device_id_type=MESH,
        )

    def forward_copy(side, i, c):
        part = pl.ds(c * rows, rows)
        if i < local:
            target = win.at[i if side == 0 else 2 * local + i, part]
            arrived = d_recv_sem.at[side, i]
        else:
            target = t_recv.at[side, i - local, part]
            arrived = t_recv_sem.at[side, i - local, c]
        return pltpu.make_async_remote_copy(
            src_ref=relay.at[i, part],
            dst_ref=target,
            send_sem=forward_sem.at[i, c],
            recv_sem=arrived,
            device_id=(group, me + 4 if side == 0 else me - 4),
            device_id_type=MESH,
        )

    def pass_on(i):
        for side in range(2):
            if relays(side, i) is not None:
                @pl.when(relays(side, i))
                def _():
                    for c in range(pieces):
                        divert_copy(side, i, c).wait_recv()
                        forward_copy(side, i, c).start()

    for f in range(local):
        for side in range(2):
            if diverted(side, f) is not None:
                @pl.when(diverted(side, f))
                def _():
                    for c in range(pieces):
                        divert_copy(side, f, c).start()

            @pl.when(direct(side, f))
            def _():
                dens_copy(side, f).start()

    loads[0].wait()
    loads[1].wait()
    loads[6].wait()
    edge = 128
    eye = lax.broadcasted_iota(jnp.int32, (edge, edge), 0) == lax.broadcasted_iota(
        jnp.int32, (edge, edge), 1
    )
    for f in range(local):
        total = jnp.zeros((1, cmap.shape[2]), F32)
        for b in range(basis // edge):
            span = pl.ds(b * edge, edge)
            block = win[local + f, span, span].astype(F32)
            pops = jnp.sum(jnp.where(eye, block, 0.0), axis=1, keepdims=True)
            total = total + jnp.sum(pops * cmap[f, span, :].astype(F32), axis=0, keepdims=True)
        pub[f, 0:1, :] = total
        pub[f, 1:4, :] = cpos[:, f, :]
    every[me] = pub[...]

    def publish(step):
        target = lax.rem(me + step, n)
        return pltpu.make_async_remote_copy(
            src_ref=pub,
            dst_ref=every.at[me],
            send_sem=q_send_sem.at[step],
            recv_sem=q_recv_sem.at[step],
            device_id=(group, target),
            device_id_type=MESH,
        )

    def publish_start(step, carry):
        publish(step).start()
        return carry

    lax.fori_loop(1, n, publish_start, 0)

    loads[2].wait()
    loads[8].wait()
    loads[9].wait()
    live, position = [], []
    for f in range(local):
        count = pair_count[first + f]
        for k in range(slots):
            live.append(jnp.where(k < count, 1.0, 0.0).astype(F32))
            position.append(partners[k, first + f] - (me - 1) * local)
    for f in range(local):
        for k in range(slots):
            half[f * slots + k] = (
                dot(win[local + f], coup[f, k]) * live[f * slots + k]
            ).astype(BF16)

    weights = [
        [jnp.where(p == w, 1.0, 0.0).astype(F32) for p in position] for w in range(3 * local)
    ]

    def gather_terms(step, carry):
        span = pl.ds(pl.multiple_of(step * 32, 32), 32)
        for c in range(basis // 128):
            cols = pl.ds(c * 128, 128)
            pieces_here = [half[i, span, cols].astype(F32) for i in range(local * slots)]
            for w in range(3 * local):
                value = pieces_here[0] * weights[w][0]
                for i in range(1, local * slots):
                    value = value + pieces_here[i] * weights[w][i]
                value = value.astype(BF16)
                if w < local:
                    t_send[1, w, span, cols] = value
                elif w < 2 * local:
                    t_own[w - local, span, cols] = value
                else:
                    t_send[0, w - 2 * local, span, cols] = value
        return carry

    lax.fori_loop(0, basis // 32, gather_terms, 0)

    def send_terms(f):
        for side in range(2):
            if diverted(side, local + f) is not None:
                @pl.when(diverted(side, local + f))
                def _():
                    for c in range(pieces):
                        divert_copy(side, local + f, c).start()

            @pl.when(direct(side, local + f))
            def _():
                for c in range(pieces):
                    term_copy(side, f, c).start()

    pass_on(0)
    late = relays(0, 1)
    for f in range(local):
        if late is None or f == 0:
            send_terms(f)
    if late is not None:
        late = jnp.logical_or(late, relays(1, 1))

        @pl.when(jnp.logical_not(late))
        def _():
            send_terms(1)

    loads[3].wait()
    loads[4].wait()
    for f in range(local):
        own = win[local + f]
        dens_t[f] = own.T
        acc[f] = core[f].astype(F32) + dot(own, resp[f])
        acc[f] += dot_t(dens_t[f], t_own[f])

    def publish_wait(step, carry):
        publish(step).wait()
        return carry

    pass_on(1)
    if late is not None:
        @pl.when(late)
        def _():
            send_terms(1)
    lax.fori_loop(1, n, publish_wait, 0)
    loads[5].wait()
    loads[7].wait()
    for f in range(local):
        for axis in range(3):
            place[axis] = jnp.broadcast_to(gpos[axis, f : f + 1, :], (128, points)).T

        field_parts = []
        strip = 64
        for g in range(points // strip):
            span = pl.ds(g * strip, strip)
            px, py, pz = (place[axis, span, :] for axis in range(3))

            def add_source(source, total):
                for other in range(local):
                    keep = jnp.where(source * local + other == first + f, 0.0, 1.0).astype(F32)
                    rowsof = every[source, other]
                    dx = px - rowsof[1:2]
                    dy = py - rowsof[2:3]
                    dz = pz - rowsof[3:4]
                    total = total + (rowsof[0:1] * keep) * lax.rsqrt(
                        dx * dx + dy * dy + dz * dz + 1.0
                    )
                return total

            field_parts.append(lax.fori_loop(0, n, add_source, jnp.zeros((strip, 128), F32)))
        total = jnp.concatenate(field_parts, axis=0)
        field = jnp.sum(total.T, axis=0, keepdims=True)
        scaled = (gbas[f].astype(F32) * field).astype(BF16)
        acc[f] += dot_t(scaled, gbas[f])

    pass_on(2)

    for side in range(2):
        @pl.when(gets_from[side])
        def _():
            for f in range(local):
                dens_copy(side, f).wait_recv()
    for f in range(local):
        for k in range(slots):
            where = jnp.clip(position[f * slots + k], 0, 3 * local - 1)
            acc[f] += dot(half[f * slots + k], win[where])

    def result_copy(f, c):
        part = pl.ds(pl.multiple_of(c * rows, rows), rows)
        return pltpu.make_async_copy(acc.at[f, :, part], fock.at[f, :, part], out_sem.at[f, c])

    for f in range(local):
        def add_piece(c, carry):
            part = pl.ds(pl.multiple_of(c * rows, rows), rows)
            for side in range(2):
                @pl.when(gets_from[side])
                def _():
                    term_copy(side, f, c).wait_recv()
                    acc[f, :, part] += dot_t(dens_t[f], t_recv[side, f, part, :])
            result_copy(f, c).start()
            return carry

        lax.fori_loop(0, pieces, add_piece, 0)

    for side in range(2):
        for i in range(2 * local):
            @pl.when(direct(side, i))
            def _():
                if i < local:
                    dens_copy(side, i).wait_send()
                else:
                    for c in range(pieces):
                        term_copy(side, i - local, c).wait_send()

            if diverted(side, i) is not None:
                @pl.when(diverted(side, i))
                def _():
                    for c in range(pieces):
                        divert_copy(side, i, c).wait_send()

                @pl.when(relays(side, i))
                def _():
                    for c in range(pieces):
                        forward_copy(side, i, c).wait_send()
    for f in range(local):
        for c in range(pieces):
            result_copy(f, c).wait()


def body(
    density, hcore, kernel, coupling, partners, pair_count, charge_map, charge_pos, grid_pos, grid_basis
):
    n = lax.axis_size("frag")
    local, basis, _ = density.shape
    slots = coupling.shape[1]
    points = grid_pos.shape[2]
    charges = charge_map.shape[2]
    rows = 128
    pieces = basis // rows
    hbm = pl.BlockSpec(memory_space=pltpu.HBM)
    square = (basis, basis)
    dma = pltpu.SemaphoreType.DMA
    return pl.pallas_call(
        functools.partial(fock_kernel, n, rows),
        out_shape=jax.ShapeDtypeStruct((local,) + square, F32),
        in_specs=[hbm] * 10,
        out_specs=hbm,
        scratch_shapes=[
            pltpu.VMEM((3 * local,) + square, BF16),
            pltpu.VMEM((local, slots) + square, BF16),
            pltpu.VMEM((local,) + square, BF16),
            pltpu.VMEM((local,) + square, BF16),
            pltpu.VMEM((local, basis, charges), BF16),
            pltpu.VMEM((local, basis, points), BF16),
            pltpu.VMEM((local * slots,) + square, BF16),
            pltpu.VMEM((2, local) + square, BF16),
            pltpu.VMEM((2, local) + square, BF16),
            pltpu.VMEM((local,) + square, BF16),
            pltpu.VMEM((local,) + square, BF16),
            pltpu.VMEM((local,) + square, F32),
            pltpu.VMEM((local, 4, charges), F32),
            pltpu.VMEM((n, local, 4, charges), F32),
            pltpu.VMEM((3, points, 128), F32),
            pltpu.VMEM((3,) + square, BF16),
            pltpu.VMEM((3, local, charges), F32),
            pltpu.VMEM((3, local, points), F32),
            pltpu.SMEM(partners.shape[::-1], jnp.int32),
            pltpu.SMEM(pair_count.shape, jnp.int32),
            dma((10,)),
            dma((local, pieces)),
            dma((2, local)),
            dma((2, local)),
            dma((2, local, pieces)),
            dma((2, local, pieces)),
            dma((n,)),
            dma((n,)),
            dma((3, pieces)),
            dma((3, pieces)),
            dma((3, pieces)),
        ],
        compiler_params=pltpu.CompilerParams(
            collective_id=0, has_side_effects=True, vmem_limit_bytes=63 * 1024 * 1024
        ),
    )(partners.T, pair_count, density, hcore, kernel, coupling, charge_map,
      jnp.swapaxes(charge_pos, 0, 1), jnp.swapaxes(grid_pos, 0, 1), grid_basis)


def solution(mesh):
    split = ("groups", "frag")
    block = P(split, None, None)
    in_specs = (
        block, block, block, P(split, None, None, None), P(), P(), block, block, block, block,
    )
    return jax.shard_map(body, mesh=mesh, in_specs=in_specs, out_specs=block, check_vma=False)
```
